32 devices in a mesh: groups: 2 (over x), dev: 16 (over z, y, core).
Axes of the slice: x: 2, y: 2, z: 4, core: 2. Of those that a mesh axis runs over, the one named last changes fastest.
Arguments:
- inputs: bfloat16 [8192, 4096], P(('groups', 'dev')), parts along dimension 0, may hold values from -6 to 6
- query_cot: bfloat16 [8192, 4096], P(('groups', 'dev')), parts along dimension 0, may hold values from -0.59765625 to 0.59765625
- value_cot: bfloat16 [8192, 1024], P(('groups', 'dev')), parts along dimension 0, may hold values from -0.59765625 to 0.59765625
- block_adapter: int32 [64, 1], P(('groups', 'dev')), parts along dimension 0, may hold values from 0 to 15
- query_down: bfloat16 [32, 64, 4096], P(('groups', 'dev')), parts along dimension 0, may hold values from -0.09375 to 0.09375
- query_up: bfloat16 [32, 64, 4096], P(('groups', 'dev')), parts along dimension 0, may hold values from -0.75 to 0.75
- value_down: bfloat16 [32, 64, 4096], P(('groups', 'dev')), parts along dimension 0, may hold values from -0.09375 to 0.09375
- value_up: bfloat16 [32, 64, 1024], P(('groups', 'dev')), parts along dimension 0, may hold values from -0.75 to 0.75
Outputs:
- input_grad: bfloat16 [8192, 4096], P(('groups', 'dev')), parts along dimension 0
- qdown_grad: bfloat16 [32, 64, 4096], P(('groups', 'dev')), parts along dimension 0
- qup_grad: bfloat16 [32, 64, 4096], P(('groups', 'dev')), parts along dimension 0
- vdown_grad: bfloat16 [32, 64, 4096], P(('groups', 'dev')), parts along dimension 0
- vup_grad: bfloat16 [32, 64, 1024], P(('groups', 'dev')), parts along dimension 0
The draws below stay inside these ranges and needn't reach their ends.
There are 2 independent parts, one for each index of `groups`. The reference program is written for one: setup_inputs(seed, part) draws one part's arguments, and reference() takes and returns one part's arrays. A program takes and returns all parts, laid end to end along the dimension named above; each array names one. Nothing has to cross between parts.
Inputs may be any that keep to these rules, and one draw needn't show every extreme that they name: `block_adapter`: every adapter is named by some block.
All inputs are finite; a program needn't handle non-finite values.
Results may differ from the reference program's by a relative error of at most 0.0058.
Values may be sent and summed in bfloat16 or wider, within the bound.
A program may use at most 64 MiB of HBM per device.

```python
import jax
import jax.numpy as jnp
from jax import lax

D = 4096
DQ = 4096
DV = 1024
R = 64
BLOCK = 128
TOKENS = 4096
BLOCKS = 32
ADAPTERS = 16


def block_scale(own_key, extent, shards, smallest, top_value):
    gain = 1.0
    for position, shards_of in shards:
        draws = jax.random.uniform(jax.random.fold_in(jax.random.fold_in(own_key, 6), position), (shards_of,), jnp.float32, smallest / len(shards), top_value / len(shards))
        gain = gain * jnp.repeat(jnp.exp(draws), extent[position] // shards_of).reshape((-1,) + (1,) * (len(extent) - 1 - position))
    return gain


def distinct(stream_key, rows, count, top, lift):
    ranking = jax.random.permutation(jax.random.fold_in(stream_key, 1), count)
    boost = ranking
    for power in range(3):
        boost = boost * boost // count
    boost = boost * lift // count
    chance = jax.random.randint(jax.random.fold_in(stream_key, 2), (rows, count), 0, 4096) + boost
    holders = jax.random.permutation(jax.random.fold_in(stream_key, 3), rows)[jnp.arange(count) % rows]
    chance = jnp.where(jnp.arange(rows)[:, None] == holders[None, :], 1 << 14, chance)
    score = chance * count + jnp.arange(count)
    return lax.top_k(score.astype(jnp.int32), top)[1].astype(jnp.int32)


def gaussian(rng, extent, scale, most, split=(), kind=jnp.bfloat16):
    drawn = jax.random.normal(rng, extent, jnp.float32) * scale
    if len(split) > 0:
        drawn = block_scale(rng, extent, split, -0.22, 0.18) * drawn
    return jnp.clip(drawn, min=-most, max=most).astype(kind)


def setup_inputs(seed: int = 0, part: int = 0) -> dict:
    seeds = jax.random.split(jax.random.key(seed), 9)
    part_keys = jax.random.split(jax.random.fold_in(seeds[8], part), 9)
    return {
        "inputs": gaussian(part_keys[0], (TOKENS, D), 1.0, 6.0, ((0, 16),)),
        "query_cot": gaussian(part_keys[1], (TOKENS, DQ), 0.1, 0.59765625, ((0, 16),)),
        "value_cot": gaussian(part_keys[2], (TOKENS, DV), 0.1, 0.59765625, ((0, 16),)),
        "block_adapter": distinct(part_keys[3], BLOCKS, ADAPTERS, 1, 1024),
        "query_down": gaussian(part_keys[4], (ADAPTERS, R, D), D ** -0.5, 0.09375, ((0, 16),)),
        "query_up": gaussian(part_keys[5], (ADAPTERS, R, DQ), R ** -0.5, 0.75, ((0, 16),)),
        "value_down": gaussian(part_keys[6], (ADAPTERS, R, D), D ** -0.5, 0.09375, ((0, 16),)),
        "value_up": gaussian(part_keys[7], (ADAPTERS, R, DV), R ** -0.5, 0.75, ((0, 16),)),
    }


adapter_scale = 2.0


def matrix_product(form, left, right):
    return jnp.einsum(form, left.astype(jnp.float32), right.astype(jnp.float32), precision=lax.Precision.HIGHEST)


def reference(inputs, query_cot, value_cot, block_adapter, query_down, query_up, value_down, value_up):
    count = inputs.shape[0] // BLOCK
    ids = block_adapter[:, 0]
    x_blocks = inputs.reshape(count, BLOCK, D)
    query_gradient_blocks = query_cot.reshape(count, BLOCK, DQ)
    value_gradient_blocks = value_cot.reshape(count, BLOCK, DV)
    sel_aq = query_down[ids]
    sel_av = value_down[ids]
    selected_query_up = query_up[ids]
    selected_value_up = value_up[ids]
    query_lowrank = matrix_product("btd,brd->btr", x_blocks, sel_aq).astype(jnp.bfloat16)
    value_lowrank = matrix_product("btd,brd->btr", x_blocks, sel_av).astype(jnp.bfloat16)
    query_backward = (adapter_scale * matrix_product("muv,mdv->mud", query_gradient_blocks, selected_query_up)).astype(jnp.bfloat16)
    value_backward = (adapter_scale * matrix_product("muv,mdv->mud", value_gradient_blocks, selected_value_up)).astype(jnp.bfloat16)
    input_grad = (matrix_product("btr,brd->btd", query_backward, sel_aq) + matrix_product("btr,brd->btd", value_backward, sel_av)).astype(jnp.bfloat16)
    term_aq = matrix_product("btr,btd->brd", query_backward, x_blocks).astype(jnp.bfloat16)
    term_av = matrix_product("btr,btd->brd", value_backward, x_blocks).astype(jnp.bfloat16)
    query_up_contribution = (adapter_scale * matrix_product("jvh,jvw->jhw", query_lowrank, query_gradient_blocks)).astype(jnp.bfloat16)
    value_up_contribution = (adapter_scale * matrix_product("jvh,jvw->jhw", value_lowrank, value_gradient_blocks)).astype(jnp.bfloat16)
    onehot = (ids[None, :] == jnp.arange(query_down.shape[0], dtype=jnp.int32)[:, None]).astype(jnp.float32)
    grads = [matrix_product("ab,brw->arw", onehot, term).astype(jnp.bfloat16) for term in (term_aq, query_up_contribution, term_av, value_up_contribution)]
    return input_grad.reshape(inputs.shape[0], D), grads[0], grads[1], grads[2], grads[3]
```

```python
import functools

import jax
import jax.numpy as jnp
from jax import lax
from jax.experimental import pallas as pl
from jax.experimental.pallas import tpu as pltpu
from jax.sharding import PartitionSpec as P

BLOCK = 128
ROWS = 16
LANES = 128
QD, VD, QU, VU = range(4)

adapter_scale = 2.0


def dot(left, right, dims):
    return lax.dot_general(left, right, (dims, ((), ())), preferred_element_type=jnp.float32)


def kernel(
    n, rank, per_dev, widths,
    ids_ref, x_ref, qc_ref, vc_ref, qd_ref, vd_ref, qu_ref, vu_ref,
    grad_ref, oqd_ref, ovd_ref, oqu_ref, ovu_ref,
    ids_v, ids_s, prev_s, last_s,
    hold_qd, hold_vd, hold_qu, hold_vu,
    stage_qd, stage_vd, stage_qu, stage_vu,
    tile_d, tile_qu, tile_vu, term_d, term_qu, term_vu,
    recv_qd, recv_vd, recv_qu, recv_vu,
    sum_qd, sum_vd, sum_qu, sum_vu,
    chain, chain_v, back_s,
    send_sem, recv_sem, id_send, id_recv, own_sem,
):
    group, me = lax.axis_index("groups"), lax.axis_index("dev")
    row_groups = rank // ROWS
    column_groups = n // row_groups
    share = [w // column_groups for w in widths]
    own = (qd_ref, vd_ref, qu_ref, vu_ref)
    out = (oqd_ref, ovd_ref, oqu_ref, ovu_ref)
    hold = (hold_qd, hold_vd, hold_qu, hold_vu)
    stage = (stage_qd, stage_vd, stage_qu, stage_vu)
    tile = (tile_d, tile_d, tile_qu, tile_vu)
    term = (term_d, term_d, term_qu, term_vu)
    recv = (recv_qd, recv_vd, recv_qu, recv_vu)
    sums = (sum_qd, sum_vd, sum_qu, sum_vu)
    chains = (chain, chain, chain, chain_v)
    base = (0, rank, 0, 0)

    def peer_of(off):
        return lax.rem(me + off, n)

    def source_of(off):
        return lax.rem(me + n - off, n)

    def rows(d, start):
        return pl.ds(pl.multiple_of(lax.div(d, column_groups) * ROWS + start, ROWS), ROWS)

    def columns(d, c):
        return pl.ds(pl.multiple_of(lax.rem(d, column_groups) * share[c], LANES), share[c])

    def remote(src, dst, phase, c, off, peer):
        return pltpu.make_async_remote_copy(
            src_ref=src, dst_ref=dst,
            send_sem=send_sem.at[phase, c, off], recv_sem=recv_sem.at[phase, c, off],
            device_id=(group, peer), device_id_type=pl.DeviceIdType.MESH,
        )

    def source(phase, c, d):
        if phase == 0:
            return own[c].at[0, rows(d, 0), columns(d, c)]
        if phase == 1:
            return stage[c].at[d]
        if phase == 2:
            return term[c].at[:, rows(d, base[c]), columns(d, c)]
        return sums[c].at[d]

    def target(phase, c, d):
        if phase == 0:
            return hold[c].at[d]
        if phase == 1:
            return tile[c].at[:, rows(d, base[c]), columns(d, c)]
        if phase == 2:
            return recv[c].at[d]
        return out[c].at[0, rows(d, 0), columns(d, c)]

    def each_peer(body):
        def step(off, carry):
            body(off)
            return carry

        lax.fori_loop(1, n, step, 0)

    def send(phase, c):
        each_peer(
            lambda off: remote(
                source(phase, c, peer_of(off)), target(phase, c, me), phase, c, off, peer_of(off)
            ).start()
        )
        pltpu.make_async_copy(source(phase, c, me), target(phase, c, me), own_sem.at[phase, c]).start()

    def arrive(phase, c):
        pltpu.make_async_copy(source(phase, c, me), target(phase, c, me), own_sem.at[phase, c]).wait()
        each_peer(
            lambda off: remote(
                source(phase, c, me), target(phase, c, source_of(off)), phase, c, off, peer_of(off)
            ).wait_recv()
        )

    def drain(phase, c):
        each_peer(
            lambda off: remote(
                source(phase, c, peer_of(off)), target(phase, c, me), phase, c, off, peer_of(off)
            ).wait_send()
        )

    def id_copy(off, slot):
        return pltpu.make_async_remote_copy(
            src_ref=ids_ref, dst_ref=ids_v.at[slot],
            send_sem=id_send.at[off], recv_sem=id_recv.at[off],
            device_id=(group, peer_of(off)), device_id_type=pl.DeviceIdType.MESH,
        )

    barrier = pltpu.get_barrier_semaphore()
    each_peer(
        lambda off: pl.semaphore_signal(
            barrier, inc=1, device_id=(group, peer_of(off)), device_id_type=pl.DeviceIdType.MESH
        )
    )
    pl.semaphore_wait(barrier, n - 1)

    each_peer(lambda off: id_copy(off, me).start())
    for c in (QD, VD, QU, VU):
        send(0, c)
    ids_v[me] = ids_ref[...]
    each_peer(lambda off: id_copy(off, source_of(off)).wait_recv())
    fetch = pltpu.make_async_copy(ids_v, ids_s, id_recv.at[0])
    fetch.start()
    fetch.wait()

    def pick(c):
        def step(d, carry):
            for k in range(per_dev):
                stage[c][d, k] = hold[c][ids_s[d, k, 0]]
            return carry

        lax.fori_loop(0, n, step, 0)

    for c in (QD, VD, QU, VU):
        arrive(0, c)
        pick(c)
        send(1, c)

    blocks = n * per_dev

    def id_of(b):
        return ids_s[lax.div(b, per_dev), lax.rem(b, per_dev), 0]

    def find_prev(b, carry):
        mine = id_of(b)
        prev_s[b] = lax.fori_loop(
            0, b, lambda j, found: jnp.where(id_of(j) == mine, j + 1, found), jnp.int32(0)
        )
        return carry

    lax.fori_loop(0, blocks, find_prev, 0)

    def find_last(a, carry):
        last_s[a] = lax.fori_loop(
            0, blocks, lambda j, found: jnp.where(id_of(j) == a, j + 1, found), jnp.int32(0)
        )
        return carry

    lax.fori_loop(0, n, find_last, 0)

    def slabs(width):
        size = 512 if width % 512 == 0 else LANES
        return width // size, size

    def contract(tile_ref, k, token_ref):
        width = token_ref.shape[2]
        count, size = slabs(width)

        def step(i, total):
            cols = pl.ds(pl.multiple_of(i * size, LANES), size)
            return total + dot(tile_ref[k, :, cols], token_ref[k, :, cols], ((1,), (1,)))

        return lax.fori_loop(
            0, count, step, jnp.zeros((tile_ref.shape[1], BLOCK), jnp.float32)
        )

    def expand(left, token_ref, k, target_ref, scale):
        count, size = slabs(token_ref.shape[2])

        def step(i, carry):
            cols = pl.ds(pl.multiple_of(i * size, LANES), size)
            value = dot(left, token_ref[k, :, cols], ((1,), (0,)))
            if scale is not None:
                value = scale * value
            target_ref[k, :, cols] = value.astype(jnp.bfloat16)
            return carry

        lax.fori_loop(0, count, step, 0)

    arrive(1, QD)
    arrive(1, VD)
    for k in range(per_dev):
        low = contract(tile_d, k, x_ref).astype(jnp.bfloat16)
        expand(low[:rank], qc_ref, k, term_qu, adapter_scale)
        expand(low[rank:], vc_ref, k, term_vu, adapter_scale)
    send(2, QU)
    send(2, VU)
    arrive(1, QU)
    arrive(1, VU)
    for k in range(per_dev):
        back_s[k, :rank] = adapter_scale * contract(tile_qu, k, qc_ref)
        back_s[k, rank:] = adapter_scale * contract(tile_vu, k, vc_ref)
        expand(back_s[k].astype(jnp.bfloat16), x_ref, k, term_d, None)
    send(2, QD)
    send(2, VD)

    def reduce(c):
        s = chains[c]
        s[0] = jnp.zeros(s.shape[1:], jnp.float32)

        def step(b, carry):
            piece = recv[c][lax.div(b, per_dev), lax.rem(b, per_dev)].astype(jnp.float32)
            s[b + 1] = piece + s[prev_s[b]]
            return carry

        lax.fori_loop(0, blocks, step, 0)

        def close(a, carry):
            sums[c][a] = s[last_s[a]].astype(jnp.bfloat16)
            return carry

        lax.fori_loop(0, n, close, 0)

    for c in (QU, VU):
        arrive(2, c)
        reduce(c)
        send(3, c)
    for k in range(per_dev):
        back = back_s[k].T.astype(jnp.bfloat16)
        expand(back, tile_d, k, grad_ref, None)
    for c in (QD, VD):
        arrive(2, c)
        reduce(c)
        send(3, c)
    each_peer(lambda off: id_copy(off, me).wait_send())
    for phase in range(3):
        for c in range(4):
            drain(phase, c)
    for c in (QU, VU, QD, VD):
        arrive(3, c)
        drain(3, c)


def per_device(
    inputs, query_cot, value_cot, block_adapter, query_down, query_up, value_down, value_up
):
    n = lax.axis_size("dev")
    rows, width = inputs.shape
    per_dev = rows // BLOCK
    rank = query_down.shape[1]
    column_groups = n // (rank // ROWS)

    def padded(w):
        return column_groups * max(LANES, w // column_groups)

    def spread(a):
        w = a.shape[-1]
        if padded(w) == w:
            return a
        parts = a.reshape(a.shape[:-1] + (column_groups, w // column_groups))
        extra = padded(w) // column_groups - w // column_groups
        parts = jnp.pad(parts, [(0, 0)] * (parts.ndim - 1) + [(0, extra)])
        return parts.reshape(a.shape[:-1] + (padded(w),))

    def unspread(a, w):
        if a.shape[-1] == w:
            return a
        parts = a.reshape(a.shape[:-1] + (column_groups, -1))
        return parts[..., : w // column_groups].reshape(a.shape[:-1] + (w,))

    vwidth = value_cot.shape[1]
    value_up, value_cot = spread(value_up), spread(value_cot)
    vpad = value_cot.shape[1]
    qwidth = query_cot.shape[1]
    widths = (width, width, qwidth, vpad)
    share = [w // column_groups for w in widths]
    ids = jnp.pad(
        jnp.broadcast_to(block_adapter, (per_dev, LANES)), ((0, -per_dev % 8), (0, 0))
    )
    bf, f32 = jnp.bfloat16, jnp.float32
    blocks = n * per_dev
    scratch = [
        pltpu.VMEM((n,) + ids.shape, jnp.int32),
        pltpu.SMEM((n,) + ids.shape, jnp.int32),
        pltpu.SMEM((blocks,), jnp.int32),
        pltpu.SMEM((n,), jnp.int32),
    ]
    scratch += [pltpu.VMEM((n, ROWS, s), bf) for s in share]
    scratch += [pltpu.VMEM((n, per_dev, ROWS, s), bf) for s in share]
    for _ in range(2):
        scratch += [
            pltpu.VMEM((per_dev, 2 * rank, width), bf),
            pltpu.VMEM((per_dev, rank, qwidth), bf),
            pltpu.VMEM((per_dev, rank, vpad), bf),
        ]
    scratch += [pltpu.VMEM((n, per_dev, ROWS, s), bf) for s in share]
    scratch += [pltpu.VMEM((n, ROWS, s), bf) for s in share]
    scratch += [
        pltpu.VMEM((blocks + 1, ROWS, share[QU]), f32),
        pltpu.VMEM((blocks + 1, ROWS, share[VU]), f32),
        pltpu.VMEM((per_dev, 2 * rank, BLOCK), f32),
        pltpu.SemaphoreType.DMA((4, 4, n)),
        pltpu.SemaphoreType.DMA((4, 4, n)),
        pltpu.SemaphoreType.DMA((n,)),
        pltpu.SemaphoreType.DMA((n,)),
        pltpu.SemaphoreType.DMA((4, 4)),
    ]
    vmem = pl.BlockSpec(memory_space=pltpu.VMEM)
    grad, qdown, vdown, qup, vup = pl.pallas_call(
        functools.partial(kernel, n, rank, per_dev, widths),
        out_shape=(
            jax.ShapeDtypeStruct((per_dev, BLOCK, width), bf),
            jax.ShapeDtypeStruct((1, rank, width), bf),
            jax.ShapeDtypeStruct((1, rank, width), bf),
            jax.ShapeDtypeStruct((1, rank, qwidth), bf),
            jax.ShapeDtypeStruct((1, rank, vpad), bf),
        ),
        in_specs=[vmem] * 8,
        out_specs=[vmem] * 5,
        scratch_shapes=scratch,
        compiler_params=pltpu.CompilerParams(
            collective_id=0, has_side_effects=True, vmem_limit_bytes=52 * 1024 * 1024
        ),
    )(
        ids,
        inputs.reshape(per_dev, BLOCK, width),
        query_cot.reshape(per_dev, BLOCK, qwidth),
        value_cot.reshape(per_dev, BLOCK, vpad),
        query_down,
        value_down,
        query_up,
        value_up,
    )
    return (grad.reshape(rows, width), qdown, qup, vdown, unspread(vup, vwidth))


def solution(mesh):
    rows = P(("groups", "dev"), None)
    factors = P(("groups", "dev"), None, None)
    return jax.shard_map(
        per_device,
        mesh=mesh,
        in_specs=(rows, rows, rows, rows, factors, factors, factors, factors),
        out_specs=(rows, factors, factors, factors, factors),
        check_vma=False,
    )
```

```python
import functools

import jax
import jax.numpy as jnp
from jax import lax
from jax.experimental import pallas as pl
from jax.experimental.pallas import tpu as pltpu
from jax.sharding import PartitionSpec as P

BLOCK = 128
ROWS = 16
LANES = 128
QD, VD, QU, VU = range(4)

adapter_scale = 2.0


def dot(left, right, dims):
    return lax.dot_general(left, right, (dims, ((), ())), preferred_element_type=jnp.float32)


def kernel(
    n, half, rank, per_dev, widths,
    ids_ref, x_ref, qc_ref, vc_ref, qd_ref, vd_ref, qu_ref, vu_ref,
    grad_ref, oqd_ref, ovd_ref, oqu_ref, ovu_ref,
    ids_v, ids_s, prev_s, last_s,
    hold_qd, hold_vd, hold_qu, hold_vu,
    stage_qd, stage_vd, stage_qu, stage_vu,
    tile_d, tile_qu, tile_vu, term_d, term_qu, term_vu,
    recv_qd, recv_vd, recv_qu, recv_vu,
    sum_qd, sum_vd, sum_qu, sum_vu,
    home_qd, home_vd, home_qu, home_vu,
    chain, chain_v, back_s,
    send_sem, recv_sem, id_send, id_recv, own_sem,
):
    group, me = lax.axis_index("groups"), lax.axis_index("dev")
    row_groups = rank // ROWS
    column_groups = half // row_groups
    side, spot = lax.div(me, half), lax.rem(me, half)
    share = [w // column_groups for w in widths]
    own = (qd_ref, vd_ref, qu_ref, vu_ref)
    out = (oqd_ref, ovd_ref, oqu_ref, ovu_ref)
    hold = (hold_qd, hold_vd, hold_qu, hold_vu)
    stage = (stage_qd, stage_vd, stage_qu, stage_vu)
    tile = (tile_d, tile_d, tile_qu, tile_vu)
    term = (term_d, term_d, term_qu, term_vu)
    recv = (recv_qd, recv_vd, recv_qu, recv_vu)
    sums = (sum_qd, sum_vd, sum_qu, sum_vu)
    home = (home_qd, home_vd, home_qu, home_vu)
    chains = (chain, chain, chain, chain_v)
    base = (0, rank, 0, 0)

    def peer_of(phase, off):
        if phase in (1, 2):
            return side * half + lax.rem(spot + off, half)
        return lax.rem(me + off, n)

    def source_of(phase, off):
        if phase in (1, 2):
            return side * half + lax.rem(spot + half - off, half)
        return lax.rem(me + n - off, n)

    def rows(d, start):
        return pl.ds(pl.multiple_of(lax.div(lax.rem(d, half), column_groups) * ROWS + start, ROWS), ROWS)

    def columns(d, c):
        return pl.ds(pl.multiple_of(lax.rem(d, column_groups) * share[c], LANES), share[c])

    def remote(src, dst, phase, c, off, peer):
        return pltpu.make_async_remote_copy(
            src_ref=src, dst_ref=dst,
            send_sem=send_sem.at[phase, c, off], recv_sem=recv_sem.at[phase, c, off],
            device_id=(group, peer), device_id_type=pl.DeviceIdType.MESH,
        )

    def source(phase, c, d):
        if phase == 0:
            return own[c].at[0, rows(d, 0), columns(d, c)]
        if phase == 1:
            return stage[c].at[lax.rem(d, half)]
        if phase == 2:
            return term[c].at[:, rows(d, base[c]), columns(d, c)]
        return sums[c].at[d]

    def target(phase, c, d):
        if phase == 0:
            return hold[c].at[d]
        if phase == 1:
            return tile[c].at[:, rows(d, base[c]), columns(d, c)]
        if phase == 2:
            return recv[c].at[lax.rem(d, half)]
        return home[c].at[lax.div(d, half), rows(d, 0), columns(d, c)]

    def each_peer(phase, body):
        def step(off, carry):
            body(off)
            return carry

        lax.fori_loop(1, half if phase in (1, 2) else n, step, 0)

    def send(phase, c):
        def step(off):
            peer = peer_of(phase, off)
            remote(source(phase, c, peer), target(phase, c, me), phase, c, off, peer).start()

        each_peer(phase, step)
        pltpu.make_async_copy(source(phase, c, me), target(phase, c, me), own_sem.at[phase, c]).start()

    def arrive(phase, c):
        pltpu.make_async_copy(source(phase, c, me), target(phase, c, me), own_sem.at[phase, c]).wait()

        def step(off):
            landed = target(phase, c, source_of(phase, off))
            remote(source(phase, c, me), landed, phase, c, off, peer_of(phase, off)).wait_recv()

        each_peer(phase, step)

    def drain(phase, c):
        def step(off):
            peer = peer_of(phase, off)
            remote(source(phase, c, peer), target(phase, c, me), phase, c, off, peer).wait_send()

        each_peer(phase, step)

    def id_copy(off, slot):
        return pltpu.make_async_remote_copy(
            src_ref=ids_ref, dst_ref=ids_v.at[slot],
            send_sem=id_send.at[off], recv_sem=id_recv.at[off],
            device_id=(group, peer_of(0, off)), device_id_type=pl.DeviceIdType.MESH,
        )

    barrier = pltpu.get_barrier_semaphore()
    each_peer(
        0,
        lambda off: pl.semaphore_signal(
            barrier, inc=1, device_id=(group, peer_of(0, off)), device_id_type=pl.DeviceIdType.MESH
        ),
    )
    pl.semaphore_wait(barrier, n - 1)

    each_peer(0, lambda off: id_copy(off, me).start())
    for c in (QD, VD, QU, VU):
        send(0, c)
    ids_v[me] = ids_ref[...]
    each_peer(0, lambda off: id_copy(off, source_of(0, off)).wait_recv())
    fetch = pltpu.make_async_copy(ids_v, ids_s, id_recv.at[0])
    fetch.start()
    fetch.wait()

    def pick(c):
        def step(d, carry):
            for k in range(per_dev):
                stage[c][d, k] = hold[c][ids_s[side * half + d, k, 0]]
            return carry

        lax.fori_loop(0, half, step, 0)

    for c in (QD, VD, QU, VU):
        arrive(0, c)
        pick(c)
        send(1, c)

    blocks = half * per_dev

    def id_of(b):
        return ids_s[side * half + lax.div(b, per_dev), lax.rem(b, per_dev), 0]

    def find_prev(b, carry):
        mine = id_of(b)
        prev_s[b] = lax.fori_loop(
            0, b, lambda j, found: jnp.where(id_of(j) == mine, j + 1, found), jnp.int32(0)
        )
        return carry

    lax.fori_loop(0, blocks, find_prev, 0)

    def find_last(a, carry):
        last_s[a] = lax.fori_loop(
            0, blocks, lambda j, found: jnp.where(id_of(j) == a, j + 1, found), jnp.int32(0)
        )
        return carry

    lax.fori_loop(0, n, find_last, 0)

    def slabs(width):
        size = 512 if width % 512 == 0 else LANES
        return width // size, size

    def contract(tile_ref, k, token_ref):
        width = token_ref.shape[2]
        count, size = slabs(width)

        def step(i, total):
            cols = pl.ds(pl.multiple_of(i * size, LANES), size)
            return total + dot(tile_ref[k, :, cols], token_ref[k, :, cols], ((1,), (1,)))

        return lax.fori_loop(
            0, count, step, jnp.zeros((tile_ref.shape[1], BLOCK), jnp.float32)
        )

    def expand(left, token_ref, k, target_ref, scale):
        count, size = slabs(token_ref.shape[2])

        def step(i, carry):
            cols = pl.ds(pl.multiple_of(i * size, LANES), size)
            value = dot(left, token_ref[k, :, cols], ((1,), (0,)))
            if scale is not None:
                value = scale * value
            target_ref[k, :, cols] = value.astype(jnp.bfloat16)
            return carry

        lax.fori_loop(0, count, step, 0)

    arrive(1, QD)
    arrive(1, VD)
    for k in range(per_dev):
        low = contract(tile_d, k, x_ref).astype(jnp.bfloat16)
        expand(low[:rank], qc_ref, k, term_qu, adapter_scale)
        expand(low[rank:], vc_ref, k, term_vu, adapter_scale)
    send(2, QU)
    send(2, VU)
    arrive(1, QU)
    arrive(1, VU)
    for k in range(per_dev):
        back_s[k, :rank] = adapter_scale * contract(tile_qu, k, qc_ref)
        back_s[k, rank:] = adapter_scale * contract(tile_vu, k, vc_ref)
        expand(back_s[k].astype(jnp.bfloat16), x_ref, k, term_d, None)
    send(2, QD)
    send(2, VD)

    def reduce(c):
        s = chains[c]
        s[0] = jnp.zeros(s.shape[1:], jnp.float32)

        def step(b, carry):
            piece = recv[c][lax.div(b, per_dev), lax.rem(b, per_dev)].astype(jnp.float32)
            s[b + 1] = piece + s[prev_s[b]]
            return carry

        lax.fori_loop(0, blocks, step, 0)

        def close(a, carry):
            sums[c][a] = s[last_s[a]].astype(jnp.bfloat16)
            return carry

        lax.fori_loop(0, n, close, 0)

    for c in (QU, VU):
        arrive(2, c)
        reduce(c)
        send(3, c)
    for k in range(per_dev):
        back = back_s[k].T.astype(jnp.bfloat16)
        expand(back, tile_d, k, grad_ref, None)
    for c in (QD, VD):
        arrive(2, c)
        reduce(c)
        send(3, c)
    each_peer(0, lambda off: id_copy(off, me).wait_send())
    for phase in range(3):
        for c in range(4):
            drain(phase, c)
    for c in (QU, VU, QD, VD):
        arrive(3, c)
        drain(3, c)
        count, size = slabs(widths[c])

        def add(i, carry):
            cols = pl.ds(pl.multiple_of(i * size, LANES), size)
            total = home[c][0, :, cols].astype(jnp.float32)
            for h in range(1, n // half):
                total += home[c][h, :, cols].astype(jnp.float32)
            out[c][0, :, cols] = total.astype(jnp.bfloat16)
            return carry

        lax.fori_loop(0, count, add, 0)


def per_device(
    inputs, query_cot, value_cot, block_adapter, query_down, query_up, value_down, value_up
):
    n = lax.axis_size("dev")
    rows, width = inputs.shape
    per_dev = rows // BLOCK
    rank = query_down.shape[1]
    half = n // 2
    column_groups = half // (rank // ROWS)

    def padded(w):
        return column_groups * max(LANES, w // column_groups)

    def spread(a):
        w = a.shape[-1]
        if padded(w) == w:
            return a
        parts = a.reshape(a.shape[:-1] + (column_groups, w // column_groups))
        extra = padded(w) // column_groups - w // column_groups
        parts = jnp.pad(parts, [(0, 0)] * (parts.ndim - 1) + [(0, extra)])
        return parts.reshape(a.shape[:-1] + (padded(w),))

    def unspread(a, w):
        if a.shape[-1] == w:
            return a
        parts = a.reshape(a.shape[:-1] + (column_groups, -1))
        return parts[..., : w // column_groups].reshape(a.shape[:-1] + (w,))

    vwidth = value_cot.shape[1]
    value_up, value_cot = spread(value_up), spread(value_cot)
    vpad = value_cot.shape[1]
    qwidth = query_cot.shape[1]
    widths = (width, width, qwidth, vpad)
    share = [w // column_groups for w in widths]
    ids = jnp.pad(
        jnp.broadcast_to(block_adapter, (per_dev, LANES)), ((0, -per_dev % 8), (0, 0))
    )
    bf, f32 = jnp.bfloat16, jnp.float32
    blocks = half * per_dev
    scratch = [
        pltpu.VMEM((n,) + ids.shape, jnp.int32),
        pltpu.SMEM((n,) + ids.shape, jnp.int32),
        pltpu.SMEM((blocks,), jnp.int32),
        pltpu.SMEM((n,), jnp.int32),
    ]
    scratch += [pltpu.VMEM((n, ROWS, s), bf) for s in share]
    scratch += [pltpu.VMEM((half, per_dev, ROWS, s), bf) for s in share]
    for _ in range(2):
        scratch += [
            pltpu.VMEM((per_dev, 2 * rank, width), bf),
            pltpu.VMEM((per_dev, rank, qwidth), bf),
            pltpu.VMEM((per_dev, rank, vpad), bf),
        ]
    scratch += [pltpu.VMEM((half, per_dev, ROWS, s), bf) for s in share]
    scratch += [pltpu.VMEM((n, ROWS, s), bf) for s in share]
    scratch += [pltpu.VMEM((n // half, rank, w), bf) for w in widths]
    scratch += [
        pltpu.VMEM((blocks + 1, ROWS, share[QU]), f32),
        pltpu.VMEM((blocks + 1, ROWS, share[VU]), f32),
        pltpu.VMEM((per_dev, 2 * rank, BLOCK), f32),
        pltpu.SemaphoreType.DMA((4, 4, n)),
        pltpu.SemaphoreType.DMA((4, 4, n)),
        pltpu.SemaphoreType.DMA((n,)),
        pltpu.SemaphoreType.DMA((n,)),
        pltpu.SemaphoreType.DMA((4, 4)),
    ]
    vmem = pl.BlockSpec(memory_space=pltpu.VMEM)
    grad, qdown, vdown, qup, vup = pl.pallas_call(
        functools.partial(kernel, n, half, rank, per_dev, widths),
        out_shape=(
            jax.ShapeDtypeStruct((per_dev, BLOCK, width), bf),
            jax.ShapeDtypeStruct((1, rank, width), bf),
            jax.ShapeDtypeStruct((1, rank, width), bf),
            jax.ShapeDtypeStruct((1, rank, qwidth), bf),
            jax.ShapeDtypeStruct((1, rank, vpad), bf),
        ),
        in_specs=[vmem] * 8,
        out_specs=[vmem] * 5,
        scratch_shapes=scratch,
        compiler_params=pltpu.CompilerParams(
            collective_id=0, has_side_effects=True, vmem_limit_bytes=52 * 1024 * 1024
        ),
    )(
        ids,
        inputs.reshape(per_dev, BLOCK, width),
        query_cot.reshape(per_dev, BLOCK, qwidth),
        value_cot.reshape(per_dev, BLOCK, vpad),
        query_down,
        value_down,
        query_up,
        value_up,
    )
    return (grad.reshape(rows, width), qdown, qup, vdown, unspread(vup, vwidth))


def solution(mesh):
    rows = P(("groups", "dev"), None)
    factors = P(("groups", "dev"), None, None)
    return jax.shard_map(
        per_device,
        mesh=mesh,
        in_specs=(rows, rows, rows, rows, factors, factors, factors, factors),
        out_specs=(rows, factors, factors, factors, factors),
        check_vma=False,
    )
```

```python
import functools

import jax
import jax.numpy as jnp
from jax import lax
from jax.experimental import pallas as pl
from jax.experimental.pallas import tpu as pltpu
from jax.sharding import PartitionSpec as P

BLOCK = 128
ROWS = 16
LANES = 128
QD, VD, QU, VU = range(4)

adapter_scale = 2.0


def dot(left, right, dims):
    return lax.dot_general(left, right, (dims, ((), ())), preferred_element_type=jnp.float32)


def kernel(
    n, half, rank, per_dev, widths,
    ids_ref, x_ref, qc_ref, vc_ref, qd_ref, vd_ref, qu_ref, vu_ref,
    grad_ref, oqd_ref, ovd_ref, oqu_ref, ovu_ref,
    ids_v, ids_s, prev_s, last_s,
    hold_qd, hold_vd, hold_qu, hold_vu,
    stage_qd, stage_vd, stage_qu, stage_vu,
    tile_d, tile_qu, tile_vu, term_d, term_qu, term_vu,
    recv_qd, recv_vd, recv_qu, recv_vu,
    sum_qd, sum_vd, sum_qu, sum_vu,
    home_qd, home_vd, home_qu, home_vu,
    chain, chain_v, back_s,
    send_sem, recv_sem, id_send, id_recv, own_sem,
):
    group, me = lax.axis_index("groups"), lax.axis_index("dev")
    row_groups = rank // ROWS
    column_groups = half // row_groups
    side, spot = lax.div(me, half), lax.rem(me, half)
    share = [w // column_groups for w in widths]
    own = (qd_ref, vd_ref, qu_ref, vu_ref)
    out = (oqd_ref, ovd_ref, oqu_ref, ovu_ref)
    hold = (hold_qd, hold_vd, hold_qu, hold_vu)
    stage = (stage_qd, stage_vd, stage_qu, stage_vu)
    tile = (tile_d, tile_d, tile_qu, tile_vu)
    term = (term_d, term_d, term_qu, term_vu)
    recv = (recv_qd, recv_vd, recv_qu, recv_vu)
    sums = (sum_qd, sum_vd, sum_qu, sum_vu)
    home = (home_qd, home_vd, home_qu, home_vu)
    chains = (chain, chain, chain, chain_v)
    base = (0, rank, 0, 0)

    def peer_of(phase, off):
        if phase in (1, 2):
            return side * half + lax.rem(spot + off, half)
        return lax.rem(me + off, n)

    def source_of(phase, off):
        if phase in (1, 2):
            return side * half + lax.rem(spot + half - off, half)
        return lax.rem(me + n - off, n)

    def rows(d, start):
        return pl.ds(pl.multiple_of(lax.div(lax.rem(d, half), column_groups) * ROWS + start, ROWS), ROWS)

    def columns(d, c):
        return pl.ds(pl.multiple_of(lax.rem(d, column_groups) * share[c], LANES), share[c])

    def remote(src, dst, phase, c, off, peer):
        return pltpu.make_async_remote_copy(
            src_ref=src, dst_ref=dst,
            send_sem=send_sem.at[phase, c, off], recv_sem=recv_sem.at[phase, c, off],
            device_id=(group, peer), device_id_type=pl.DeviceIdType.MESH,
        )

    def source(phase, c, d):
        if phase == 0:
            return own[c].at[0, rows(d, 0), columns(d, c)]
        if phase == 1:
            return stage[c].at[lax.rem(d, half)]
        if phase == 2:
            return term[c].at[:, rows(d, base[c]), columns(d, c)]
        return sums[c].at[d]

    def target(phase, c, d):
        if phase == 0:
            return hold[c].at[d]
        if phase == 1:
            return tile[c].at[:, rows(d, base[c]), columns(d, c)]
        if phase == 2:
            return recv[c].at[lax.rem(d, half)]
        return home[c].at[lax.div(d, half), rows(d, 0), columns(d, c)]

    def each_peer(phase, body):
        def step(off, carry):
            body(off)
            return carry

        lax.fori_loop(1, half if phase in (1, 2) else n, step, 0)

    def send(phase, c):
        def step(off):
            peer = peer_of(phase, off)
            remote(source(phase, c, peer), target(phase, c, me), phase, c, off, peer).start()

        each_peer(phase, step)
        pltpu.make_async_copy(source(phase, c, me), target(phase, c, me), own_sem.at[phase, c]).start()

    def arrive(phase, c):
        pltpu.make_async_copy(source(phase, c, me), target(phase, c, me), own_sem.at[phase, c]).wait()

        def step(off):
            landed = target(phase, c, source_of(phase, off))
            remote(source(phase, c, me), landed, phase, c, off, peer_of(phase, off)).wait_recv()

        each_peer(phase, step)

    def drain(phase, c):
        def step(off):
            peer = peer_of(phase, off)
            remote(source(phase, c, peer), target(phase, c, me), phase, c, off, peer).wait_send()

        each_peer(phase, step)

    def id_copy(off, slot):
        return pltpu.make_async_remote_copy(
            src_ref=ids_ref, dst_ref=ids_v.at[slot],
            send_sem=id_send.at[off], recv_sem=id_recv.at[off],
            device_id=(group, peer_of(0, off)), device_id_type=pl.DeviceIdType.MESH,
        )

    barrier = pltpu.get_barrier_semaphore()
    each_peer(
        0,
        lambda off: pl.semaphore_signal(
            barrier, inc=1, device_id=(group, peer_of(0, off)), device_id_type=pl.DeviceIdType.MESH
        ),
    )
    pl.semaphore_wait(barrier, n - 1)

    each_peer(0, lambda off: id_copy(off, me).start())
    send(0, QD)
    send(0, VD)
    ids_v[me] = ids_ref[...]
    each_peer(0, lambda off: id_copy(off, source_of(0, off)).wait_recv())
    fetch = pltpu.make_async_copy(ids_v, ids_s, id_recv.at[0])
    fetch.start()
    fetch.wait()

    def pick(c):
        def step(d, carry):
            for k in range(per_dev):
                stage[c][d, k] = hold[c][ids_s[side * half + d, k, 0]]
            return carry

        lax.fori_loop(0, half, step, 0)

    for c in (QD, VD, QU, VU):
        arrive(0, c)
        pick(c)
        send(1, c)
        if c + 2 <= VU:
            send(0, c + 2)

    blocks = half * per_dev

    def id_of(b):
        return ids_s[side * half + lax.div(b, per_dev), lax.rem(b, per_dev), 0]

    def find_prev(b, carry):
        mine = id_of(b)
        prev_s[b] = lax.fori_loop(
            0, b, lambda j, found: jnp.where(id_of(j) == mine, j + 1, found), jnp.int32(0)
        )
        return carry

    lax.fori_loop(0, blocks, find_prev, 0)

    def find_last(a, carry):
        last_s[a] = lax.fori_loop(
            0, blocks, lambda j, found: jnp.where(id_of(j) == a, j + 1, found), jnp.int32(0)
        )
        return carry

    lax.fori_loop(0, n, find_last, 0)

    def slabs(width):
        size = 512 if width % 512 == 0 else LANES
        return width // size, size

    def contract(tile_ref, k, token_ref):
        width = token_ref.shape[2]
        count, size = slabs(width)

        def step(i, total):
            cols = pl.ds(pl.multiple_of(i * size, LANES), size)
            return total + dot(tile_ref[k, :, cols], token_ref[k, :, cols], ((1,), (1,)))

        return lax.fori_loop(
            0, count, step, jnp.zeros((tile_ref.shape[1], BLOCK), jnp.float32)
        )

    def expand(left, token_ref, k, target_ref, scale, start=0):
        count, size = slabs(token_ref.shape[2])

        def step(i, carry):
            cols = pl.ds(pl.multiple_of(i * size, LANES), size)
            value = dot(left, token_ref[k, :, cols], ((1,), (0,)))
            if scale is not None:
                value = scale * value
            target_ref[k, pl.ds(start, left.shape[0]), cols] = value.astype(jnp.bfloat16)
            return carry

        lax.fori_loop(0, count, step, 0)

    arrive(1, QD)
    arrive(1, VD)
    for k in range(per_dev):
        low = contract(tile_d, k, x_ref).astype(jnp.bfloat16)
        expand(low[:rank], qc_ref, k, term_qu, adapter_scale)
        expand(low[rank:], vc_ref, k, term_vu, adapter_scale)
    send(2, QU)
    send(2, VU)
    def reduce(c):
        s = chains[c]
        s[0] = jnp.zeros(s.shape[1:], jnp.float32)

        def step(b, carry):
            piece = recv[c][lax.div(b, per_dev), lax.rem(b, per_dev)].astype(jnp.float32)
            s[b + 1] = piece + s[prev_s[b]]
            return carry

        lax.fori_loop(0, blocks, step, 0)

        def close(a, carry):
            sums[c][a] = s[last_s[a]].astype(jnp.bfloat16)
            return carry

        lax.fori_loop(0, n, close, 0)

    def backward(c, up, cot_ref):
        arrive(1, up)
        for k in range(per_dev):
            back = adapter_scale * contract(tile[up], k, cot_ref)
            back_s[k, pl.ds(base[c], rank)] = back
            expand(back.astype(jnp.bfloat16), x_ref, k, term_d, None, base[c])
        send(2, c)

    def total(c):
        arrive(2, c)
        reduce(c)
        send(3, c)

    backward(QD, QU, qc_ref)
    total(QU)
    backward(VD, VU, vc_ref)
    total(VU)
    total(QD)
    for k in range(per_dev):
        back = back_s[k].T.astype(jnp.bfloat16)
        expand(back, tile_d, k, grad_ref, None)
    total(VD)
    each_peer(0, lambda off: id_copy(off, me).wait_send())
    for phase in range(3):
        for c in range(4):
            drain(phase, c)
    for c in (QU, VU, QD, VD):
        arrive(3, c)
        drain(3, c)
        count, size = slabs(widths[c])

        def add(i, carry):
            cols = pl.ds(pl.multiple_of(i * size, LANES), size)
            total = home[c][0, :, cols].astype(jnp.float32)
            for h in range(1, n // half):
                total += home[c][h, :, cols].astype(jnp.float32)
            out[c][0, :, cols] = total.astype(jnp.bfloat16)
            return carry

        lax.fori_loop(0, count, add, 0)


def per_device(
    inputs, query_cot, value_cot, block_adapter, query_down, query_up, value_down, value_up
):
    n = lax.axis_size("dev")
    rows, width = inputs.shape
    per_dev = rows // BLOCK
    rank = query_down.shape[1]
    half = n // 2
    column_groups = half // (rank // ROWS)

    def padded(w):
        return column_groups * max(LANES, w // column_groups)

    def spread(a):
        w = a.shape[-1]
        if padded(w) == w:
            return a
        parts = a.reshape(a.shape[:-1] + (column_groups, w // column_groups))
        extra = padded(w) // column_groups - w // column_groups
        parts = jnp.pad(parts, [(0, 0)] * (parts.ndim - 1) + [(0, extra)])
        return parts.reshape(a.shape[:-1] + (padded(w),))

    def unspread(a, w):
        if a.shape[-1] == w:
            return a
        parts = a.reshape(a.shape[:-1] + (column_groups, -1))
        return parts[..., : w // column_groups].reshape(a.shape[:-1] + (w,))

    vwidth = value_cot.shape[1]
    value_up, value_cot = spread(value_up), spread(value_cot)
    vpad = value_cot.shape[1]
    qwidth = query_cot.shape[1]
    widths = (width, width, qwidth, vpad)
    share = [w // column_groups for w in widths]
    ids = jnp.pad(
        jnp.broadcast_to(block_adapter, (per_dev, LANES)), ((0, -per_dev % 8), (0, 0))
    )
    bf, f32 = jnp.bfloat16, jnp.float32
    blocks = half * per_dev
    scratch = [
        pltpu.VMEM((n,) + ids.shape, jnp.int32),
        pltpu.SMEM((n,) + ids.shape, jnp.int32),
        pltpu.SMEM((blocks,), jnp.int32),
        pltpu.SMEM((n,), jnp.int32),
    ]
    scratch += [pltpu.VMEM((n, ROWS, s), bf) for s in share]
    scratch += [pltpu.VMEM((half, per_dev, ROWS, s), bf) for s in share]
    for _ in range(2):
        scratch += [
            pltpu.VMEM((per_dev, 2 * rank, width), bf),
            pltpu.VMEM((per_dev, rank, qwidth), bf),
            pltpu.VMEM((per_dev, rank, vpad), bf),
        ]
    scratch += [pltpu.VMEM((half, per_dev, ROWS, s), bf) for s in share]
    scratch += [pltpu.VMEM((n, ROWS, s), bf) for s in share]
    scratch += [pltpu.VMEM((n // half, rank, w), bf) for w in widths]
    scratch += [
        pltpu.VMEM((blocks + 1, ROWS, share[QU]), f32),
        pltpu.VMEM((blocks + 1, ROWS, share[VU]), f32),
        pltpu.VMEM((per_dev, 2 * rank, BLOCK), f32),
        pltpu.SemaphoreType.DMA((4, 4, n)),
        pltpu.SemaphoreType.DMA((4, 4, n)),
        pltpu.SemaphoreType.DMA((n,)),
        pltpu.SemaphoreType.DMA((n,)),
        pltpu.SemaphoreType.DMA((4, 4)),
    ]
    vmem = pl.BlockSpec(memory_space=pltpu.VMEM)
    grad, qdown, vdown, qup, vup = pl.pallas_call(
        functools.partial(kernel, n, half, rank, per_dev, widths),
        out_shape=(
            jax.ShapeDtypeStruct((per_dev, BLOCK, width), bf),
            jax.ShapeDtypeStruct((1, rank, width), bf),
            jax.ShapeDtypeStruct((1, rank, width), bf),
            jax.ShapeDtypeStruct((1, rank, qwidth), bf),
            jax.ShapeDtypeStruct((1, rank, vpad), bf),
        ),
        in_specs=[vmem] * 8,
        out_specs=[vmem] * 5,
        scratch_shapes=scratch,
        compiler_params=pltpu.CompilerParams(
            collective_id=0, has_side_effects=True, vmem_limit_bytes=52 * 1024 * 1024
        ),
    )(
        ids,
        inputs.reshape(per_dev, BLOCK, width),
        query_cot.reshape(per_dev, BLOCK, qwidth),
        value_cot.reshape(per_dev, BLOCK, vpad),
        query_down,
        value_down,
        query_up,
        value_up,
    )
    return (grad.reshape(rows, width), qdown, qup, vdown, unspread(vup, vwidth))


def solution(mesh):
    rows = P(("groups", "dev"), None)
    factors = P(("groups", "dev"), None, None)
    return jax.shard_map(
        per_device,
        mesh=mesh,
        in_specs=(rows, rows, rows, rows, factors, factors, factors, factors),
        out_specs=(rows, factors, factors, factors, factors),
        check_vma=False,
    )
```

```python
import functools
import math

import jax
import jax.numpy as jnp
from jax import lax
from jax.experimental import pallas as pl
from jax.experimental.pallas import tpu as pltpu
from jax.sharding import PartitionSpec as P

BLOCK = 128
ROWS = 16
LANES = 128
QD, VD, QU, VU = range(4)

adapter_scale = 2.0


def dot(left, right, dims):
    return lax.dot_general(left, right, (dims, ((), ())), preferred_element_type=jnp.float32)


def kernel(
    n, half, rank, per_dev, widths,
    ids_ref, x_ref, qc_ref, vc_ref, qd_ref, vd_ref, qu_ref, vu_ref,
    grad_ref, oqd_ref, ovd_ref, oqu_ref, ovu_ref,
    ids_v, ids_s, prev_s, last_s,
    hold_qd, hold_vd, hold_qu, hold_vu,
    stage_qd, stage_vd, stage_qu, stage_vu,
    tile_d, tile_qu, tile_vu, term_d, term_qu, term_vu,
    recv_qd, recv_vd, recv_qu, recv_vu,
    sum_qd, sum_vd, sum_qu, sum_vu,
    home_qd, home_vd, home_qu, home_vu,
    chain, chain_v, back_s,
    send_sem, recv_sem, id_send, id_recv, own_sem,
):
    group, me = lax.axis_index("groups"), lax.axis_index("dev")
    row_groups = rank // ROWS
    column_groups = half // row_groups
    side, spot = lax.div(me, half), lax.rem(me, half)
    share = [w // column_groups for w in widths]
    own = (qd_ref, vd_ref, qu_ref, vu_ref)
    out = (oqd_ref, ovd_ref, oqu_ref, ovu_ref)
    hold = (hold_qd, hold_vd, hold_qu, hold_vu)
    stage = (stage_qd, stage_vd, stage_qu, stage_vu)
    tile = (tile_d, tile_d, tile_qu, tile_vu)
    term = (term_d, term_d, term_qu, term_vu)
    recv = (recv_qd, recv_vd, recv_qu, recv_vu)
    sums = (sum_qd, sum_vd, sum_qu, sum_vu)
    home = (home_qd, home_vd, home_qu, home_vu)
    chains = (chain, chain, chain, chain_v)
    base = (0, rank, 0, 0)

    stride = next(s for s in range(n // 3, 0, -1) if math.gcd(s, n) == 1)
    near_stride = next(s for s in range(half // 2, 0, -1) if math.gcd(s, half) == 1)

    def peer_of(phase, off):
        if phase in (1, 2):
            return side * half + lax.rem(spot + off * near_stride, half)
        return lax.rem(me + off * stride, n)

    def source_of(phase, off):
        if phase in (1, 2):
            return side * half + lax.rem(spot + half * near_stride - off * near_stride, half)
        return lax.rem(me + n * stride - off * stride, n)

    def rows(d, start):
        return pl.ds(pl.multiple_of(lax.div(lax.rem(d, half), column_groups) * ROWS + start, ROWS), ROWS)

    def columns(d, c):
        return pl.ds(pl.multiple_of(lax.rem(d, column_groups) * share[c], LANES), share[c])

    def remote(src, dst, phase, c, off, peer):
        return pltpu.make_async_remote_copy(
            src_ref=src, dst_ref=dst,
            send_sem=send_sem.at[phase, c, off], recv_sem=recv_sem.at[phase, c, off],
            device_id=(group, peer), device_id_type=pl.DeviceIdType.MESH,
        )

    def source(phase, c, d):
        if phase == 0:
            return own[c].at[0, rows(d, 0), columns(d, c)]
        if phase == 1:
            return stage[c].at[lax.rem(d, half)]
        if phase == 2:
            return term[c].at[:, rows(d, base[c]), columns(d, c)]
        return sums[c].at[d]

    def target(phase, c, d):
        if phase == 0:
            return hold[c].at[d]
        if phase == 1:
            return tile[c].at[:, rows(d, base[c]), columns(d, c)]
        if phase == 2:
            return recv[c].at[lax.rem(d, half)]
        return home[c].at[lax.div(d, half), rows(d, 0), columns(d, c)]

    def each_peer(phase, body):
        def step(off, carry):
            body(off)
            return carry

        lax.fori_loop(1, half if phase in (1, 2) else n, step, 0)

    def send(phase, c):
        def step(off):
            peer = peer_of(phase, off)
            remote(source(phase, c, peer), target(phase, c, me), phase, c, off, peer).start()

        each_peer(phase, step)
        pltpu.make_async_copy(source(phase, c, me), target(phase, c, me), own_sem.at[phase, c]).start()

    def arrive(phase, c):
        pltpu.make_async_copy(source(phase, c, me), target(phase, c, me), own_sem.at[phase, c]).wait()

        def step(off):
            landed = target(phase, c, source_of(phase, off))
            remote(source(phase, c, me), landed, phase, c, off, peer_of(phase, off)).wait_recv()

        each_peer(phase, step)

    def drain(phase, c):
        def step(off):
            peer = peer_of(phase, off)
            remote(source(phase, c, peer), target(phase, c, me), phase, c, off, peer).wait_send()

        each_peer(phase, step)

    def id_copy(off, slot):
        return pltpu.make_async_remote_copy(
            src_ref=ids_ref, dst_ref=ids_v.at[slot],
            send_sem=id_send.at[off], recv_sem=id_recv.at[off],
            device_id=(group, peer_of(0, off)), device_id_type=pl.DeviceIdType.MESH,
        )

    barrier = pltpu.get_barrier_semaphore()
    each_peer(
        0,
        lambda off: pl.semaphore_signal(
            barrier, inc=1, device_id=(group, peer_of(0, off)), device_id_type=pl.DeviceIdType.MESH
        ),
    )
    pl.semaphore_wait(barrier, n - 1)

    each_peer(0, lambda off: id_copy(off, me).start())
    for c in (QD, VD, QU, VU):
        send(0, c)
    ids_v[me] = ids_ref[...]
    each_peer(0, lambda off: id_copy(off, source_of(0, off)).wait_recv())
    fetch = pltpu.make_async_copy(ids_v, ids_s, id_recv.at[0])
    fetch.start()
    fetch.wait()

    def pick(c):
        def step(d, carry):
            for k in range(per_dev):
                stage[c][d, k] = hold[c][ids_s[side * half + d, k, 0]]
            return carry

        lax.fori_loop(0, half, step, 0)

    for c in (QD, VD, QU, VU):
        arrive(0, c)
        pick(c)
        send(1, c)

    blocks = half * per_dev

    def id_of(b):
        return ids_s[side * half + lax.div(b, per_dev), lax.rem(b, per_dev), 0]

    def find_prev(b, carry):
        mine = id_of(b)
        prev_s[b] = lax.fori_loop(
            0, b, lambda j, found: jnp.where(id_of(j) == mine, j + 1, found), jnp.int32(0)
        )
        return carry

    lax.fori_loop(0, blocks, find_prev, 0)

    def find_last(a, carry):
        last_s[a] = lax.fori_loop(
            0, blocks, lambda j, found: jnp.where(id_of(j) == a, j + 1, found), jnp.int32(0)
        )
        return carry

    lax.fori_loop(0, n, find_last, 0)

    def slabs(width):
        size = 512 if width % 512 == 0 else LANES
        return width // size, size

    def contract(tile_ref, k, token_ref):
        width = token_ref.shape[2]
        count, size = slabs(width)

        def step(i, total):
            cols = pl.ds(pl.multiple_of(i * size, LANES), size)
            return total + dot(tile_ref[k, :, cols], token_ref[k, :, cols], ((1,), (1,)))

        return lax.fori_loop(
            0, count, step, jnp.zeros((tile_ref.shape[1], BLOCK), jnp.float32)
        )

    def expand(left, token_ref, k, target_ref, scale):
        count, size = slabs(token_ref.shape[2])

        def step(i, carry):
            cols = pl.ds(pl.multiple_of(i * size, LANES), size)
            value = dot(left, token_ref[k, :, cols], ((1,), (0,)))
            if scale is not None:
                value = scale * value
            target_ref[k, :, cols] = value.astype(jnp.bfloat16)
            return carry

        lax.fori_loop(0, count, step, 0)

    arrive(1, QD)
    arrive(1, VD)
    for k in range(per_dev):
        low = contract(tile_d, k, x_ref).astype(jnp.bfloat16)
        expand(low[:rank], qc_ref, k, term_qu, adapter_scale)
        expand(low[rank:], vc_ref, k, term_vu, adapter_scale)
    send(2, QU)
    send(2, VU)
    arrive(1, QU)
    arrive(1, VU)
    for k in range(per_dev):
        back_s[k, :rank] = adapter_scale * contract(tile_qu, k, qc_ref)
        back_s[k, rank:] = adapter_scale * contract(tile_vu, k, vc_ref)
        expand(back_s[k].astype(jnp.bfloat16), x_ref, k, term_d, None)
    send(2, QD)
    send(2, VD)

    def reduce(c):
        s = chains[c]
        s[0] = jnp.zeros(s.shape[1:], jnp.float32)

        def step(b, carry):
            piece = recv[c][lax.div(b, per_dev), lax.rem(b, per_dev)].astype(jnp.float32)
            s[b + 1] = piece + s[prev_s[b]]
            return carry

        lax.fori_loop(0, blocks, step, 0)

        def close(a, carry):
            sums[c][a] = s[last_s[a]].astype(jnp.bfloat16)
            return carry

        lax.fori_loop(0, n, close, 0)

    for c in (QU, VU):
        arrive(2, c)
        reduce(c)
        send(3, c)
    for k in range(per_dev):
        back = back_s[k].T.astype(jnp.bfloat16)
        expand(back, tile_d, k, grad_ref, None)
    for c in (QD, VD):
        arrive(2, c)
        reduce(c)
        send(3, c)
    each_peer(0, lambda off: id_copy(off, me).wait_send())
    for phase in range(3):
        for c in range(4):
            drain(phase, c)
    for c in (QU, VU, QD, VD):
        arrive(3, c)
        drain(3, c)
        count, size = slabs(widths[c])

        def add(i, carry):
            cols = pl.ds(pl.multiple_of(i * size, LANES), size)
            total = home[c][0, :, cols].astype(jnp.float32)
            for h in range(1, n // half):
                total += home[c][h, :, cols].astype(jnp.float32)
            out[c][0, :, cols] = total.astype(jnp.bfloat16)
            return carry

        lax.fori_loop(0, count, add, 0)


def per_device(
    inputs, query_cot, value_cot, block_adapter, query_down, query_up, value_down, value_up
):
    n = lax.axis_size("dev")
    rows, width = inputs.shape
    per_dev = rows // BLOCK
    rank = query_down.shape[1]
    half = n // 2
    column_groups = half // (rank // ROWS)

    def padded(w):
        return column_groups * max(LANES, w // column_groups)

    def spread(a):
        w = a.shape[-1]
        if padded(w) == w:
            return a
        parts = a.reshape(a.shape[:-1] + (column_groups, w // column_groups))
        extra = padded(w) // column_groups - w // column_groups
        parts = jnp.pad(parts, [(0, 0)] * (parts.ndim - 1) + [(0, extra)])
        return parts.reshape(a.shape[:-1] + (padded(w),))

    def unspread(a, w):
        if a.shape[-1] == w:
            return a
        parts = a.reshape(a.shape[:-1] + (column_groups, -1))
        return parts[..., : w // column_groups].reshape(a.shape[:-1] + (w,))

    vwidth = value_cot.shape[1]
    value_up, value_cot = spread(value_up), spread(value_cot)
    vpad = value_cot.shape[1]
    qwidth = query_cot.shape[1]
    widths = (width, width, qwidth, vpad)
    share = [w // column_groups for w in widths]
    ids = jnp.pad(
        jnp.broadcast_to(block_adapter, (per_dev, LANES)), ((0, -per_dev % 8), (0, 0))
    )
    bf, f32 = jnp.bfloat16, jnp.float32
    blocks = half * per_dev
    scratch = [
        pltpu.VMEM((n,) + ids.shape, jnp.int32),
        pltpu.SMEM((n,) + ids.shape, jnp.int32),
        pltpu.SMEM((blocks,), jnp.int32),
        pltpu.SMEM((n,), jnp.int32),
    ]
    scratch += [pltpu.VMEM((n, ROWS, s), bf) for s in share]
    scratch += [pltpu.VMEM((half, per_dev, ROWS, s), bf) for s in share]
    for _ in range(2):
        scratch += [
            pltpu.VMEM((per_dev, 2 * rank, width), bf),
            pltpu.VMEM((per_dev, rank, qwidth), bf),
            pltpu.VMEM((per_dev, rank, vpad), bf),
        ]
    scratch += [pltpu.VMEM((half, per_dev, ROWS, s), bf) for s in share]
    scratch += [pltpu.VMEM((n, ROWS, s), bf) for s in share]
    scratch += [pltpu.VMEM((n // half, rank, w), bf) for w in widths]
    scratch += [
        pltpu.VMEM((blocks + 1, ROWS, share[QU]), f32),
        pltpu.VMEM((blocks + 1, ROWS, share[VU]), f32),
        pltpu.VMEM((per_dev, 2 * rank, BLOCK), f32),
        pltpu.SemaphoreType.DMA((4, 4, n)),
        pltpu.SemaphoreType.DMA((4, 4, n)),
        pltpu.SemaphoreType.DMA((n,)),
        pltpu.SemaphoreType.DMA((n,)),
        pltpu.SemaphoreType.DMA((4, 4)),
    ]
    vmem = pl.BlockSpec(memory_space=pltpu.VMEM)
    grad, qdown, vdown, qup, vup = pl.pallas_call(
        functools.partial(kernel, n, half, rank, per_dev, widths),
        out_shape=(
            jax.ShapeDtypeStruct((per_dev, BLOCK, width), bf),
            jax.ShapeDtypeStruct((1, rank, width), bf),
            jax.ShapeDtypeStruct((1, rank, width), bf),
            jax.ShapeDtypeStruct((1, rank, qwidth), bf),
            jax.ShapeDtypeStruct((1, rank, vpad), bf),
        ),
        in_specs=[vmem] * 8,
        out_specs=[vmem] * 5,
        scratch_shapes=scratch,
        compiler_params=pltpu.CompilerParams(
            collective_id=0, has_side_effects=True, vmem_limit_bytes=52 * 1024 * 1024
        ),
    )(
        ids,
        inputs.reshape(per_dev, BLOCK, width),
        query_cot.reshape(per_dev, BLOCK, qwidth),
        value_cot.reshape(per_dev, BLOCK, vpad),
        query_down,
        value_down,
        query_up,
        value_up,
    )
    return (grad.reshape(rows, width), qdown, qup, vdown, unspread(vup, vwidth))


def solution(mesh):
    rows = P(("groups", "dev"), None)
    factors = P(("groups", "dev"), None, None)
    return jax.shard_map(
        per_device,
        mesh=mesh,
        in_specs=(rows, rows, rows, rows, factors, factors, factors, factors),
        out_specs=(rows, factors, factors, factors, factors),
        check_vma=False,
    )
```

```python
import functools

import jax
import jax.numpy as jnp
from jax import lax
from jax.experimental import pallas as pl
from jax.experimental.pallas import tpu as pltpu
from jax.sharding import PartitionSpec as P

BLOCK = 128
ROWS = 16
LANES = 128
QD, VD, QU, VU = range(4)

adapter_scale = 2.0


def dot(left, right, dims):
    return lax.dot_general(left, right, (dims, ((), ())), preferred_element_type=jnp.float32)


def kernel(
    n, half, rank, per_dev, widths,
    ids_ref, x_hbm, qc_hbm, vc_hbm, qd_ref, vd_ref, qu_ref, vu_ref,
    grad_hbm, oqd_ref, ovd_ref, oqu_ref, ovu_ref,
    ids_v, ids_s, prev_s, last_s,
    hold_qd, hold_vd, hold_qu, hold_vu,
    stage_qd, stage_vd, stage_qu, stage_vu,
    tile_d, tile_qu, tile_vu, term_d, term_qu, term_vu,
    recv_qd, recv_vd, recv_qu, recv_vu,
    sum_qd, sum_vd, sum_qu, sum_vu,
    home_qd, home_vd, home_qu, home_vu,
    chain, chain_v, back_s,
    send_sem, recv_sem, id_send, id_recv, own_sem,
    x_ref, qc_ref, vc_ref, grad_ref, local_sem,
):
    group, me = lax.axis_index("groups"), lax.axis_index("dev")
    row_groups = rank // ROWS
    column_groups = half // row_groups
    side, spot = lax.div(me, half), lax.rem(me, half)
    share = [w // column_groups for w in widths]
    own = (qd_ref, vd_ref, qu_ref, vu_ref)
    out = (oqd_ref, ovd_ref, oqu_ref, ovu_ref)
    hold = (hold_qd, hold_vd, hold_qu, hold_vu)
    stage = (stage_qd, stage_vd, stage_qu, stage_vu)
    tile = (tile_d, tile_d, tile_qu, tile_vu)
    term = (term_d, term_d, term_qu, term_vu)
    recv = (recv_qd, recv_vd, recv_qu, recv_vu)
    sums = (sum_qd, sum_vd, sum_qu, sum_vu)
    home = (home_qd, home_vd, home_qu, home_vu)
    chains = (chain, chain, chain, chain_v)
    base = (0, rank, 0, 0)

    def peer_of(phase, off):
        if phase in (1, 2):
            return side * half + lax.rem(spot + off, half)
        return lax.rem(me + off, n)

    def source_of(phase, off):
        if phase in (1, 2):
            return side * half + lax.rem(spot + half - off, half)
        return lax.rem(me + n - off, n)

    def rows(d, start):
        return pl.ds(pl.multiple_of(lax.div(lax.rem(d, half), column_groups) * ROWS + start, ROWS), ROWS)

    def columns(d, c):
        return pl.ds(pl.multiple_of(lax.rem(d, column_groups) * share[c], LANES), share[c])

    def remote(src, dst, phase, c, off, peer):
        return pltpu.make_async_remote_copy(
            src_ref=src, dst_ref=dst,
            send_sem=send_sem.at[phase, c, off], recv_sem=recv_sem.at[phase, c, off],
            device_id=(group, peer), device_id_type=pl.DeviceIdType.MESH,
        )

    def source(phase, c, d):
        if phase == 0:
            return own[c].at[0, rows(d, 0), columns(d, c)]
        if phase == 1:
            return stage[c].at[lax.rem(d, half)]
        if phase == 2:
            return term[c].at[:, rows(d, base[c]), columns(d, c)]
        return sums[c].at[d]

    def target(phase, c, d):
        if phase == 0:
            return hold[c].at[d]
        if phase == 1:
            return tile[c].at[:, rows(d, base[c]), columns(d, c)]
        if phase == 2:
            return recv[c].at[lax.rem(d, half)]
        return home[c].at[lax.div(d, half), rows(d, 0), columns(d, c)]

    def each_peer(phase, body):
        def step(off, carry):
            body(off)
            return carry

        lax.fori_loop(1, half if phase in (1, 2) else n, step, 0)

    def send(phase, c):
        def step(off):
            peer = peer_of(phase, off)
            remote(source(phase, c, peer), target(phase, c, me), phase, c, off, peer).start()

        each_peer(phase, step)
        pltpu.make_async_copy(source(phase, c, me), target(phase, c, me), own_sem.at[phase, c]).start()

    def arrive(phase, c):
        pltpu.make_async_copy(source(phase, c, me), target(phase, c, me), own_sem.at[phase, c]).wait()

        def step(off):
            landed = target(phase, c, source_of(phase, off))
            remote(source(phase, c, me), landed, phase, c, off, peer_of(phase, off)).wait_recv()

        each_peer(phase, step)

    def drain(phase, c):
        def step(off):
            peer = peer_of(phase, off)
            remote(source(phase, c, peer), target(phase, c, me), phase, c, off, peer).wait_send()

        each_peer(phase, step)

    def id_copy(off, slot):
        return pltpu.make_async_remote_copy(
            src_ref=ids_ref, dst_ref=ids_v.at[slot],
            send_sem=id_send.at[off], recv_sem=id_recv.at[off],
            device_id=(group, peer_of(0, off)), device_id_type=pl.DeviceIdType.MESH,
        )

    loads = [
        pltpu.make_async_copy(src, dst, local_sem.at[i])
        for i, (src, dst) in enumerate(((x_hbm, x_ref), (qc_hbm, qc_ref), (vc_hbm, vc_ref)))
    ]
    store = pltpu.make_async_copy(grad_ref, grad_hbm, local_sem.at[3])

    barrier = pltpu.get_barrier_semaphore()
    each_peer(
        0,
        lambda off: pl.semaphore_signal(
            barrier, inc=1, device_id=(group, peer_of(0, off)), device_id_type=pl.DeviceIdType.MESH
        ),
    )
    pl.semaphore_wait(barrier, n - 1)

    each_peer(0, lambda off: id_copy(off, me).start())
    for c in (QD, VD, QU, VU):
        send(0, c)
    for load in loads:
        load.start()
    ids_v[me] = ids_ref[...]
    each_peer(0, lambda off: id_copy(off, source_of(0, off)).wait_recv())
    fetch = pltpu.make_async_copy(ids_v, ids_s, id_recv.at[0])
    fetch.start()
    fetch.wait()

    def pick(c):
        def step(d, carry):
            for k in range(per_dev):
                stage[c][d, k] = hold[c][ids_s[side * half + d, k, 0]]
            return carry

        lax.fori_loop(0, half, step, 0)

    for c in (QD, VD, QU, VU):
        arrive(0, c)
        pick(c)
        send(1, c)

    blocks = half * per_dev

    def id_of(b):
        return ids_s[side * half + lax.div(b, per_dev), lax.rem(b, per_dev), 0]

    def find_prev(b, carry):
        mine = id_of(b)
        prev_s[b] = lax.fori_loop(
            0, b, lambda j, found: jnp.where(id_of(j) == mine, j + 1, found), jnp.int32(0)
        )
        return carry

    lax.fori_loop(0, blocks, find_prev, 0)

    def find_last(a, carry):
        last_s[a] = lax.fori_loop(
            0, blocks, lambda j, found: jnp.where(id_of(j) == a, j + 1, found), jnp.int32(0)
        )
        return carry

    lax.fori_loop(0, n, find_last, 0)

    def slabs(width):
        size = 512 if width % 512 == 0 else LANES
        return width // size, size

    def contract(tile_ref, k, token_ref):
        width = token_ref.shape[2]
        count, size = slabs(width)

        def step(i, total):
            cols = pl.ds(pl.multiple_of(i * size, LANES), size)
            return total + dot(tile_ref[k, :, cols], token_ref[k, :, cols], ((1,), (1,)))

        return lax.fori_loop(
            0, count, step, jnp.zeros((tile_ref.shape[1], BLOCK), jnp.float32)
        )

    def expand(left, token_ref, k, target_ref, scale):
        count, size = slabs(token_ref.shape[2])

        def step(i, carry):
            cols = pl.ds(pl.multiple_of(i * size, LANES), size)
            value = dot(left, token_ref[k, :, cols], ((1,), (0,)))
            if scale is not None:
                value = scale * value
            target_ref[k, :, cols] = value.astype(jnp.bfloat16)
            return carry

        lax.fori_loop(0, count, step, 0)

    for load in loads:
        load.wait()
    arrive(1, QD)
    arrive(1, VD)
    for k in range(per_dev):
        low = contract(tile_d, k, x_ref).astype(jnp.bfloat16)
        expand(low[:rank], qc_ref, k, term_qu, adapter_scale)
        expand(low[rank:], vc_ref, k, term_vu, adapter_scale)
    send(2, QU)
    send(2, VU)
    arrive(1, QU)
    arrive(1, VU)
    for k in range(per_dev):
        back_s[k, :rank] = adapter_scale * contract(tile_qu, k, qc_ref)
        back_s[k, rank:] = adapter_scale * contract(tile_vu, k, vc_ref)
        expand(back_s[k].astype(jnp.bfloat16), x_ref, k, term_d, None)
    send(2, QD)
    send(2, VD)

    def reduce(c):
        s = chains[c]
        s[0] = jnp.zeros(s.shape[1:], jnp.float32)

        def step(b, carry):
            piece = recv[c][lax.div(b, per_dev), lax.rem(b, per_dev)].astype(jnp.float32)
            s[b + 1] = piece + s[prev_s[b]]
            return carry

        lax.fori_loop(0, blocks, step, 0)

        def close(a, carry):
            sums[c][a] = s[last_s[a]].astype(jnp.bfloat16)
            return carry

        lax.fori_loop(0, n, close, 0)

    for c in (QU, VU):
        arrive(2, c)
        reduce(c)
        send(3, c)
    for k in range(per_dev):
        back = back_s[k].T.astype(jnp.bfloat16)
        expand(back, tile_d, k, grad_ref, None)
    store.start()
    for c in (QD, VD):
        arrive(2, c)
        reduce(c)
        send(3, c)
    each_peer(0, lambda off: id_copy(off, me).wait_send())
    for phase in range(3):
        for c in range(4):
            drain(phase, c)
    store.wait()
    for c in (QU, VU, QD, VD):
        arrive(3, c)
        drain(3, c)
        count, size = slabs(widths[c])

        def add(i, carry):
            cols = pl.ds(pl.multiple_of(i * size, LANES), size)
            total = home[c][0, :, cols].astype(jnp.float32)
            for h in range(1, n // half):
                total += home[c][h, :, cols].astype(jnp.float32)
            out[c][0, :, cols] = total.astype(jnp.bfloat16)
            return carry

        lax.fori_loop(0, count, add, 0)


def per_device(
    inputs, query_cot, value_cot, block_adapter, query_down, query_up, value_down, value_up
):
    n = lax.axis_size("dev")
    rows, width = inputs.shape
    per_dev = rows // BLOCK
    rank = query_down.shape[1]
    half = n // 2
    column_groups = half // (rank // ROWS)

    def padded(w):
        return column_groups * max(LANES, w // column_groups)

    def spread(a):
        w = a.shape[-1]
        if padded(w) == w:
            return a
        parts = a.reshape(a.shape[:-1] + (column_groups, w // column_groups))
        extra = padded(w) // column_groups - w // column_groups
        parts = jnp.pad(parts, [(0, 0)] * (parts.ndim - 1) + [(0, extra)])
        return parts.reshape(a.shape[:-1] + (padded(w),))

    def unspread(a, w):
        if a.shape[-1] == w:
            return a
        parts = a.reshape(a.shape[:-1] + (column_groups, -1))
        return parts[..., : w // column_groups].reshape(a.shape[:-1] + (w,))

    vwidth = value_cot.shape[1]
    value_up, value_cot = spread(value_up), spread(value_cot)
    vpad = value_cot.shape[1]
    qwidth = query_cot.shape[1]
    widths = (width, width, qwidth, vpad)
    share = [w // column_groups for w in widths]
    ids = jnp.pad(
        jnp.broadcast_to(block_adapter, (per_dev, LANES)), ((0, -per_dev % 8), (0, 0))
    )
    bf, f32 = jnp.bfloat16, jnp.float32
    blocks = half * per_dev
    scratch = [
        pltpu.VMEM((n,) + ids.shape, jnp.int32),
        pltpu.SMEM((n,) + ids.shape, jnp.int32),
        pltpu.SMEM((blocks,), jnp.int32),
        pltpu.SMEM((n,), jnp.int32),
    ]
    scratch += [pltpu.VMEM((n, ROWS, s), bf) for s in share]
    scratch += [pltpu.VMEM((half, per_dev, ROWS, s), bf) for s in share]
    for _ in range(2):
        scratch += [
            pltpu.VMEM((per_dev, 2 * rank, width), bf),
            pltpu.VMEM((per_dev, rank, qwidth), bf),
            pltpu.VMEM((per_dev, rank, vpad), bf),
        ]
    scratch += [pltpu.VMEM((half, per_dev, ROWS, s), bf) for s in share]
    scratch += [pltpu.VMEM((n, ROWS, s), bf) for s in share]
    scratch += [pltpu.VMEM((n // half, rank, w), bf) for w in widths]
    scratch += [
        pltpu.VMEM((blocks + 1, ROWS, share[QU]), f32),
        pltpu.VMEM((blocks + 1, ROWS, share[VU]), f32),
        pltpu.VMEM((per_dev, 2 * rank, BLOCK), f32),
        pltpu.SemaphoreType.DMA((4, 4, n)),
        pltpu.SemaphoreType.DMA((4, 4, n)),
        pltpu.SemaphoreType.DMA((n,)),
        pltpu.SemaphoreType.DMA((n,)),
        pltpu.SemaphoreType.DMA((4, 4)),
        pltpu.VMEM((per_dev, BLOCK, width), bf),
        pltpu.VMEM((per_dev, BLOCK, qwidth), bf),
        pltpu.VMEM((per_dev, BLOCK, vpad), bf),
        pltpu.VMEM((per_dev, BLOCK, width), bf),
        pltpu.SemaphoreType.DMA((4,)),
    ]
    vmem = pl.BlockSpec(memory_space=pltpu.VMEM)
    hbm = pl.BlockSpec(memory_space=pl.ANY)
    grad, qdown, vdown, qup, vup = pl.pallas_call(
        functools.partial(kernel, n, half, rank, per_dev, widths),
        out_shape=(
            jax.ShapeDtypeStruct((per_dev, BLOCK, width), bf),
            jax.ShapeDtypeStruct((1, rank, width), bf),
            jax.ShapeDtypeStruct((1, rank, width), bf),
            jax.ShapeDtypeStruct((1, rank, qwidth), bf),
            jax.ShapeDtypeStruct((1, rank, vpad), bf),
        ),
        in_specs=[vmem] + [hbm] * 3 + [vmem] * 4,
        out_specs=[hbm] + [vmem] * 4,
        scratch_shapes=scratch,
        compiler_params=pltpu.CompilerParams(
            collective_id=0, has_side_effects=True, vmem_limit_bytes=52 * 1024 * 1024
        ),
    )(
        ids,
        inputs.reshape(per_dev, BLOCK, width),
        query_cot.reshape(per_dev, BLOCK, qwidth),
        value_cot.reshape(per_dev, BLOCK, vpad),
        query_down,
        value_down,
        query_up,
        value_up,
    )
    return (grad.reshape(rows, width), qdown, qup, vdown, unspread(vup, vwidth))


def solution(mesh):
    rows = P(("groups", "dev"), None)
    factors = P(("groups", "dev"), None, None)
    return jax.shard_map(
        per_device,
        mesh=mesh,
        in_specs=(rows, rows, rows, rows, factors, factors, factors, factors),
        out_specs=(rows, factors, factors, factors, factors),
        check_vma=False,
    )
```

```python
import functools

import jax
import jax.numpy as jnp
from jax import lax
from jax.experimental import pallas as pl
from jax.experimental.pallas import tpu as pltpu
from jax.sharding import PartitionSpec as P

BLOCK = 128
ROWS = 16
LANES = 128
QD, VD, QU, VU = range(4)

adapter_scale = 2.0


def dot(left, right, dims):
    return lax.dot_general(left, right, (dims, ((), ())), preferred_element_type=jnp.float32)


def kernel(
    n, half, rank, per_dev, widths,
    ids_ref, x_hbm, qc_hbm, vc_hbm, qd_ref, vd_ref, qu_ref, vu_ref,
    grad_hbm, oqd_ref, ovd_ref, oqu_ref, ovu_ref,
    ids_v, ids_s, prev_s, last_s,
    hold_qd, hold_vd, hold_qu, hold_vu,
    stage_qd, stage_vd, stage_qu, stage_vu,
    tile_d, tile_qu, tile_vu, term_d, term_qu, term_vu,
    recv_qd, recv_vd, recv_qu, recv_vu,
    sum_qd, sum_vd, sum_qu, sum_vu,
    home_qd, home_vd, home_qu, home_vu,
    chain, chain_v, back_s,
    send_sem, recv_sem, id_send, id_recv, own_sem,
    x_ref, qc_ref, vc_ref, grad_ref, local_sem,
):
    group, me = lax.axis_index("groups"), lax.axis_index("dev")
    row_groups = rank // ROWS
    column_groups = half // row_groups
    side, spot = lax.div(me, half), lax.rem(me, half)
    share = [w // column_groups for w in widths]
    own = (qd_ref, vd_ref, qu_ref, vu_ref)
    out = (oqd_ref, ovd_ref, oqu_ref, ovu_ref)
    hold = (hold_qd, hold_vd, hold_qu, hold_vu)
    stage = (stage_qd, stage_vd, stage_qu, stage_vu)
    tile = (tile_d, tile_d, tile_qu, tile_vu)
    term = (term_d, term_d, term_qu, term_vu)
    recv = (recv_qd, recv_vd, recv_qu, recv_vu)
    sums = (sum_qd, sum_vd, sum_qu, sum_vu)
    home = (home_qd, home_vd, home_qu, home_vu)
    chains = (chain, chain, chain, chain_v)
    base = (0, rank, 0, 0)

    def peer_of(phase, off):
        if phase in (1, 2):
            return side * half + lax.rem(spot + off, half)
        return lax.rem(me + off, n)

    def source_of(phase, off):
        if phase in (1, 2):
            return side * half + lax.rem(spot + half - off, half)
        return lax.rem(me + n - off, n)

    def rows(d, start):
        return pl.ds(pl.multiple_of(lax.div(lax.rem(d, half), column_groups) * ROWS + start, ROWS), ROWS)

    def columns(d, c):
        return pl.ds(pl.multiple_of(lax.rem(d, column_groups) * share[c], LANES), share[c])

    def remote(src, dst, phase, c, off, peer):
        return pltpu.make_async_remote_copy(
            src_ref=src, dst_ref=dst,
            send_sem=send_sem.at[phase, c, off], recv_sem=recv_sem.at[phase, c, off],
            device_id=(group, peer), device_id_type=pl.DeviceIdType.MESH,
        )

    def source(phase, c, d):
        if phase == 0:
            return own[c].at[0, rows(d, 0), columns(d, c)]
        if phase == 1:
            return stage[c].at[lax.rem(d, half)]
        if phase == 2:
            return term[c].at[:, rows(d, base[c]), columns(d, c)]
        return sums[c].at[d]

    def target(phase, c, d):
        if phase == 0:
            return hold[c].at[d]
        if phase == 1:
            return tile[c].at[:, rows(d, base[c]), columns(d, c)]
        if phase == 2:
            return recv[c].at[lax.rem(d, half)]
        return home[c].at[lax.div(d, half), rows(d, 0), columns(d, c)]

    def each_peer(phase, body):
        def step(off, carry):
            body(off)
            return carry

        lax.fori_loop(1, half if phase in (1, 2) else n, step, 0)

    def send(phase, c):
        def step(off):
            peer = peer_of(phase, off)
            remote(source(phase, c, peer), target(phase, c, me), phase, c, off, peer).start()

        each_peer(phase, step)
        pltpu.make_async_copy(source(phase, c, me), target(phase, c, me), own_sem.at[phase, c]).start()

    def arrive(phase, c):
        pltpu.make_async_copy(source(phase, c, me), target(phase, c, me), own_sem.at[phase, c]).wait()

        def step(off):
            landed = target(phase, c, source_of(phase, off))
            remote(source(phase, c, me), landed, phase, c, off, peer_of(phase, off)).wait_recv()

        each_peer(phase, step)

    def drain(phase, c):
        def step(off):
            peer = peer_of(phase, off)
            remote(source(phase, c, peer), target(phase, c, me), phase, c, off, peer).wait_send()

        each_peer(phase, step)

    def id_copy(off, slot):
        return pltpu.make_async_remote_copy(
            src_ref=ids_ref, dst_ref=ids_v.at[slot],
            send_sem=id_send.at[off], recv_sem=id_recv.at[off],
            device_id=(group, peer_of(0, off)), device_id_type=pl.DeviceIdType.MESH,
        )

    loads = [
        pltpu.make_async_copy(src, dst, local_sem.at[i])
        for i, (src, dst) in enumerate(((x_hbm, x_ref), (qc_hbm, qc_ref), (vc_hbm, vc_ref)))
    ]
    store = pltpu.make_async_copy(grad_ref, grad_hbm, local_sem.at[3])

    barrier = pltpu.get_barrier_semaphore()
    each_peer(
        0,
        lambda off: pl.semaphore_signal(
            barrier, inc=1, device_id=(group, peer_of(0, off)), device_id_type=pl.DeviceIdType.MESH
        ),
    )
    pl.semaphore_wait(barrier, n - 1)

    each_peer(0, lambda off: id_copy(off, me).start())
    for c in (QD, VD, QU, VU):
        send(0, c)
    for load in loads:
        load.start()
    ids_v[me] = ids_ref[...]
    each_peer(0, lambda off: id_copy(off, source_of(0, off)).wait_recv())
    fetch = pltpu.make_async_copy(ids_v, ids_s, id_recv.at[0])
    fetch.start()
    fetch.wait()

    def pick(c):
        def step(d, carry):
            for k in range(per_dev):
                stage[c][d, k] = hold[c][ids_s[side * half + d, k, 0]]
            return carry

        lax.fori_loop(0, half, step, 0)

    for c in (QD, VD, QU, VU):
        arrive(0, c)
        pick(c)
        send(1, c)

    blocks = half * per_dev

    def id_of(b):
        return ids_s[side * half + lax.div(b, per_dev), lax.rem(b, per_dev), 0]

    def find_prev(b, carry):
        mine = id_of(b)
        prev_s[b] = lax.fori_loop(
            0, b, lambda j, found: jnp.where(id_of(j) == mine, j + 1, found), jnp.int32(0)
        )
        return carry

    lax.fori_loop(0, blocks, find_prev, 0)

    def find_last(a, carry):
        last_s[a] = lax.fori_loop(
            0, blocks, lambda j, found: jnp.where(id_of(j) == a, j + 1, found), jnp.int32(0)
        )
        return carry

    lax.fori_loop(0, n, find_last, 0)

    def slabs(width):
        size = 512 if width % 512 == 0 else LANES
        return width // size, size

    def contract(tile_ref, k, token_ref, start=0):
        width = token_ref.shape[2]
        count, size = slabs(width)

        def step(i, total):
            cols = pl.ds(pl.multiple_of(i * size, LANES), size)
            return total + dot(tile_ref[k, pl.ds(start, rank), cols], token_ref[k, :, cols], ((1,), (1,)))

        return lax.fori_loop(
            0, count, step, jnp.zeros((rank, BLOCK), jnp.float32)
        )

    def expand(left, token_ref, k, target_ref, scale):
        count, size = slabs(token_ref.shape[2])

        def step(i, carry):
            cols = pl.ds(pl.multiple_of(i * size, LANES), size)
            value = dot(left, token_ref[k, :, cols], ((1,), (0,)))
            if scale is not None:
                value = scale * value
            target_ref[k, :, cols] = value.astype(jnp.bfloat16)
            return carry

        lax.fori_loop(0, count, step, 0)

    for load in loads:
        load.wait()
    for c, up, cot_ref in ((QD, QU, qc_ref), (VD, VU, vc_ref)):
        arrive(1, c)
        for k in range(per_dev):
            low = contract(tile_d, k, x_ref, base[c]).astype(jnp.bfloat16)
            expand(low, cot_ref, k, term[up], adapter_scale)
        send(2, up)
    arrive(1, QU)
    arrive(1, VU)
    for k in range(per_dev):
        back_s[k, :rank] = adapter_scale * contract(tile_qu, k, qc_ref)
        back_s[k, rank:] = adapter_scale * contract(tile_vu, k, vc_ref)
        expand(back_s[k].astype(jnp.bfloat16), x_ref, k, term_d, None)
    send(2, QD)
    send(2, VD)

    def reduce(c):
        s = chains[c]
        s[0] = jnp.zeros(s.shape[1:], jnp.float32)

        def step(b, carry):
            piece = recv[c][lax.div(b, per_dev), lax.rem(b, per_dev)].astype(jnp.float32)
            s[b + 1] = piece + s[prev_s[b]]
            return carry

        lax.fori_loop(0, blocks, step, 0)

        def close(a, carry):
            sums[c][a] = s[last_s[a]].astype(jnp.bfloat16)
            return carry

        lax.fori_loop(0, n, close, 0)

    for c in (QU, VU):
        arrive(2, c)
        reduce(c)
        send(3, c)
    for k in range(per_dev):
        back = back_s[k].T.astype(jnp.bfloat16)
        expand(back, tile_d, k, grad_ref, None)
    store.start()
    for c in (QD, VD):
        arrive(2, c)
        reduce(c)
        send(3, c)
    each_peer(0, lambda off: id_copy(off, me).wait_send())
    for phase in range(3):
        for c in range(4):
            drain(phase, c)
    store.wait()
    for c in (QU, VU, QD, VD):
        arrive(3, c)
        drain(3, c)
        count, size = slabs(widths[c])

        def add(i, carry):
            cols = pl.ds(pl.multiple_of(i * size, LANES), size)
            total = home[c][0, :, cols].astype(jnp.float32)
            for h in range(1, n // half):
                total += home[c][h, :, cols].astype(jnp.float32)
            out[c][0, :, cols] = total.astype(jnp.bfloat16)
            return carry

        lax.fori_loop(0, count, add, 0)


def per_device(
    inputs, query_cot, value_cot, block_adapter, query_down, query_up, value_down, value_up
):
    n = lax.axis_size("dev")
    rows, width = inputs.shape
    per_dev = rows // BLOCK
    rank = query_down.shape[1]
    half = n // 2
    column_groups = half // (rank // ROWS)

    def padded(w):
        return column_groups * max(LANES, w // column_groups)

    def spread(a):
        w = a.shape[-1]
        if padded(w) == w:
            return a
        parts = a.reshape(a.shape[:-1] + (column_groups, w // column_groups))
        extra = padded(w) // column_groups - w // column_groups
        parts = jnp.pad(parts, [(0, 0)] * (parts.ndim - 1) + [(0, extra)])
        return parts.reshape(a.shape[:-1] + (padded(w),))

    def unspread(a, w):
        if a.shape[-1] == w:
            return a
        parts = a.reshape(a.shape[:-1] + (column_groups, -1))
        return parts[..., : w // column_groups].reshape(a.shape[:-1] + (w,))

    vwidth = value_cot.shape[1]
    value_up, value_cot = spread(value_up), spread(value_cot)
    vpad = value_cot.shape[1]
    qwidth = query_cot.shape[1]
    widths = (width, width, qwidth, vpad)
    share = [w // column_groups for w in widths]
    ids = jnp.pad(
        jnp.broadcast_to(block_adapter, (per_dev, LANES)), ((0, -per_dev % 8), (0, 0))
    )
    bf, f32 = jnp.bfloat16, jnp.float32
    blocks = half * per_dev
    scratch = [
        pltpu.VMEM((n,) + ids.shape, jnp.int32),
        pltpu.SMEM((n,) + ids.shape, jnp.int32),
        pltpu.SMEM((blocks,), jnp.int32),
        pltpu.SMEM((n,), jnp.int32),
    ]
    scratch += [pltpu.VMEM((n, ROWS, s), bf) for s in share]
    scratch += [pltpu.VMEM((half, per_dev, ROWS, s), bf) for s in share]
    for _ in range(2):
        scratch += [
            pltpu.VMEM((per_dev, 2 * rank, width), bf),
            pltpu.VMEM((per_dev, rank, qwidth), bf),
            pltpu.VMEM((per_dev, rank, vpad), bf),
        ]
    scratch += [pltpu.VMEM((half, per_dev, ROWS, s), bf) for s in share]
    scratch += [pltpu.VMEM((n, ROWS, s), bf) for s in share]
    scratch += [pltpu.VMEM((n // half, rank, w), bf) for w in widths]
    scratch += [
        pltpu.VMEM((blocks + 1, ROWS, share[QU]), f32),
        pltpu.VMEM((blocks + 1, ROWS, share[VU]), f32),
        pltpu.VMEM((per_dev, 2 * rank, BLOCK), f32),
        pltpu.SemaphoreType.DMA((4, 4, n)),
        pltpu.SemaphoreType.DMA((4, 4, n)),
        pltpu.SemaphoreType.DMA((n,)),
        pltpu.SemaphoreType.DMA((n,)),
        pltpu.SemaphoreType.DMA((4, 4)),
        pltpu.VMEM((per_dev, BLOCK, width), bf),
        pltpu.VMEM((per_dev, BLOCK, qwidth), bf),
        pltpu.VMEM((per_dev, BLOCK, vpad), bf),
        pltpu.VMEM((per_dev, BLOCK, width), bf),
        pltpu.SemaphoreType.DMA((4,)),
    ]
    vmem = pl.BlockSpec(memory_space=pltpu.VMEM)
    hbm = pl.BlockSpec(memory_space=pl.ANY)
    grad, qdown, vdown, qup, vup = pl.pallas_call(
        functools.partial(kernel, n, half, rank, per_dev, widths),
        out_shape=(
            jax.ShapeDtypeStruct((per_dev, BLOCK, width), bf),
            jax.ShapeDtypeStruct((1, rank, width), bf),
            jax.ShapeDtypeStruct((1, rank, width), bf),
            jax.ShapeDtypeStruct((1, rank, qwidth), bf),
            jax.ShapeDtypeStruct((1, rank, vpad), bf),
        ),
        in_specs=[vmem] + [hbm] * 3 + [vmem] * 4,
        out_specs=[hbm] + [vmem] * 4,
        scratch_shapes=scratch,
        compiler_params=pltpu.CompilerParams(
            collective_id=0, has_side_effects=True, vmem_limit_bytes=52 * 1024 * 1024
        ),
    )(
        ids,
        inputs.reshape(per_dev, BLOCK, width),
        query_cot.reshape(per_dev, BLOCK, qwidth),
        value_cot.reshape(per_dev, BLOCK, vpad),
        query_down,
        value_down,
        query_up,
        value_up,
    )
    return (grad.reshape(rows, width), qdown, qup, vdown, unspread(vup, vwidth))


def solution(mesh):
    rows = P(("groups", "dev"), None)
    factors = P(("groups", "dev"), None, None)
    return jax.shard_map(
        per_device,
        mesh=mesh,
        in_specs=(rows, rows, rows, rows, factors, factors, factors, factors),
        out_specs=(rows, factors, factors, factors, factors),
        check_vma=False,
    )
```
